256 devices in a mesh: energy: 8 (over y, core), rows: 32 (over z, x).
Axes of the slice: x: 4, y: 4, z: 8, core: 2. Of those that a mesh axis runs over, the one named last changes fastest.
Arguments:
- panels: bfloat16 [8, 256, 2, 128, 256], P('energy', 'rows'), may hold values from -0.029907227 to 0.029907227
- energy_weight: float32 [8], P('energy'), may hold values from 0.1 to 1
- block_orbitals: int32 [256], replicated, may hold values from 40 to 64, as said below
- pattern_columns: int32 [256, 6], P('rows'), may hold values from 0 to 255, as said below
- request_source: int32 [4096, 1], replicated, may hold values from 0 to 31; in each aligned block of 16 rows (0 to 15, 16 to 31, ...) at most 2 rows name the same one
- request_local: int32 [4096], replicated, may hold values from 0 to 7
- orbital_values: bfloat16 [4096, 384, 128], P(('energy', 'rows')), may hold values from -6 to 6
Outputs:
- density: float32 [4, 32768], P(None, ('energy', 'rows'))
The draws below stay inside these ranges and needn't reach their ends.
Inputs may be any that keep to these rules, and one draw needn't show every extreme that they name: `block_orbitals`: some block has exactly 64 live orbitals. `pattern_columns`: row i lists block i first, then 6 - 1 distinct other blocks, each within 8 blocks of i. `request_source`: among the 16 requests of one device no rows index appears more than 2 times, and some device has a rows index exactly 2 times.
All inputs are finite; a program needn't handle non-finite values.
Results may differ from the reference program's by a relative error of at most 0.0045.
Values may be sent and summed in bfloat16 or wider, within the bound.
No kernel may reach another device: no remote copies, remote signals or barrier semaphores. Data moves between devices by JAX's collectives and lax.ppermute only.
A program may use at most 128 MiB of HBM per device.

```python
import math
import jax
import jax.numpy as jnp
import numpy as np
from jax import lax

B = 64
K = 256
NNZ = 6
RB = 8
REQ_DEV = 16
CELLS_DEV = 128
ENERGIES = 8
NB = 256
CAP = 2
REQUESTS = 4096
N_ENERGY = 8
N_ROWS = 32


def draw_block_orbitals(key, part):
    count_key, full_key = jax.random.split(key)
    counts = jax.random.randint(count_key, (NB,), 5 * B // 8, B + 1)
    full_block = jax.random.randint(full_key, (), 0, NB)
    return jnp.where(jnp.arange(NB) == full_block, B, counts).astype(jnp.int32)


def draw_pattern_columns(key, part):
    score_key, sign_key = jax.random.split(key)
    scores = jax.random.randint(score_key, (NB, RB), 0, 2 ** 20) * RB + jnp.arange(RB)[None, :]
    ranking = jnp.argsort(scores, axis=1)
    magnitude = ranking[:, :NNZ - 1] + 1
    sign_pick = jax.random.randint(sign_key, (NB, NNZ - 1), 0, 2) * 2 - 1
    row_ids = jnp.arange(NB)[:, None]
    forward = row_ids + sign_pick * magnitude
    inside = (forward >= 0) & (forward < NB)
    columns = jnp.where(inside, forward, row_ids - sign_pick * magnitude)
    return jnp.concatenate([row_ids, columns], axis=1).astype(jnp.int32)


def plant(array, rng, least, largest):
    longest = array.shape.index(max(array.shape))
    spots = []
    for shift in (0, 1):
        where = [jax.random.randint(jax.random.fold_in(rng, axis), (), 0, length) for axis, length in enumerate(array.shape)]
        where[longest] = (where[longest] + shift) % array.shape[longest]
        spots.append(tuple(where))
    return array.at[spots[0]].set(least).at[spots[1]].set(largest)


def steps_of(own_key, extent, cuts, smallest, top_value):
    level = 1.0
    for position, parts in cuts:
        heights = jax.random.uniform(jax.random.fold_in(jax.random.fold_in(own_key, 6), position), (parts,), jnp.float32, smallest / len(cuts), top_value / len(cuts))
        level = level * jnp.repeat(jnp.exp(heights), extent[position] // parts).reshape((-1,) + (1,) * (len(extent) - 1 - position))
    return level


def assign_block(own_key, own, number, rows, amount, top, bound, slope):
    sequence = jax.random.permutation(own_key, amount)
    crowded, common = shares(amount, rows * top, bound, slope, True), shares(amount, rows * top, bound, slope, False)
    places = jnp.arange(amount)

    def named(sizes, turn):
        used = int((sizes > 0).sum())
        fixed = max(1, used // 4)
        moved = fixed + (places - fixed + turn * (used - fixed)) % max(1, amount - fixed)
        return jnp.zeros((amount,), jnp.int32).at[sequence[jnp.where(places < fixed, places, moved)]].set(jnp.asarray(sizes, jnp.int32))

    sizes = jnp.where(number % 4 == 0, named(crowded, number // 4), named(common, number - number // 4 - 1))
    mixed = jax.random.permutation(jax.random.fold_in(own, 3), amount)
    giver, receiver = mixed[0:amount // 2 * 2:2], mixed[1:amount // 2 * 2:2]
    slack = jnp.minimum(sizes[giver] - 1, bound - sizes[receiver]) // 2
    slack = jnp.where((giver == sequence[0]) | (receiver == sequence[0]) | (sizes[receiver] == 0), 0, jnp.maximum(slack, 0))
    moved = jax.random.randint(jax.random.fold_in(own, 4), (amount // 2,), 0, 1 << 20) % (slack + 1)
    sizes = sizes.at[giver].add(-moved).at[receiver].add(moved)
    labels = jnp.searchsorted(jnp.cumsum(sizes), jnp.arange(rows * top), side="right").astype(jnp.int32)
    grid = labels.reshape(top, rows).T
    grid = grid[jax.random.permutation(jax.random.fold_in(own, 1), rows)]
    turn = jax.random.randint(jax.random.fold_in(own, 2), (rows, 1), 0, top)
    return jnp.take_along_axis(grid, (jnp.arange(top)[None, :] + turn) % top, axis=1)


def shares(amount, total, reach, lean, full):
    weights = [(1 << 20) // math.isqrt(rank ** lean) + 1 for rank in range(1, amount + 1)]
    largest = reach if full else min(reach, max(-(-total // amount), total * weights[0] // sum(weights)))
    least = 1 if total - largest >= amount - 1 else 0
    holding, spare = [largest] + [least] * (amount - 1), total - largest - least * (amount - 1)
    while spare > 0:
        candidates = [i for i in range(1, amount) if holding[i] < largest] or [i for i in range(1, amount) if holding[i] < reach]
        mass, budget = sum([weights[i] for i in candidates]), spare
        for i in candidates:
            extra = min(reach - holding[i], max(1, budget * weights[i] // mass), spare)
            holding[i] = holding[i] + extra
            spare = spare - extra
    return np.array(holding)


def gaussian(rng, shape, width, reach, cuts=(), kind=jnp.bfloat16):
    array = width * jax.random.normal(rng, shape, jnp.float32)
    if cuts:
        array = array * steps_of(rng, shape, cuts, -0.22, 0.18)
    return jnp.clip(array, -reach, reach).astype(kind)


def setup_inputs(seed: int = 0) -> dict:
    keys = jax.random.split(jax.random.key(seed), 8)
    panels = gaussian(keys[0], (ENERGIES, NB, 2, 2 * B, K), 0.005, 0.029907227, ((0, 8), (1, 32)))
    energy_weight = jnp.clip(jnp.exp(math.log(1.0) - 2.3025851 * jax.random.uniform(keys[1], (ENERGIES,), jnp.float32) ** steps_of(keys[1], (ENERGIES,), ((0, 8),), -0.2, 0.2)), 0.1, 1.0)
    block_orbitals = draw_block_orbitals(jax.random.fold_in(keys[7], 71), 0)
    pattern_columns = draw_pattern_columns(jax.random.fold_in(keys[7], 71), 0)
    request_source_keys = jax.random.split(jax.random.fold_in(keys[4], 1), REQUESTS // REQ_DEV)
    request_source_turns = jax.random.permutation(jax.random.fold_in(keys[4], 3), REQUESTS // REQ_DEV)
    request_source = jax.vmap(lambda own, number: assign_block(jax.random.fold_in(keys[4], 2), own, number, REQ_DEV, N_ROWS, 1, CAP, 2))(request_source_keys, request_source_turns).reshape((REQUESTS, 1))
    request_local = plant(jax.random.randint(keys[5], (REQUESTS,), 0, RB), jax.random.fold_in(keys[5], 1), 0, RB - 1).astype(jnp.int32)
    orbital_values = gaussian(keys[6], (REQUESTS, NNZ * B, CELLS_DEV), 1.0, 6.0, ((0, 256),))
    return {"panels": panels, "energy_weight": energy_weight, "block_orbitals": block_orbitals, "pattern_columns": pattern_columns, "request_source": request_source, "request_local": request_local, "orbital_values": orbital_values}


def spin_parts(real_part, imag_part):
    block_width = real_part.shape[-1] // 2
    new_shape = real_part.shape[:-3] + (2, block_width, real_part.shape[-2], 2, block_width)
    real_view = real_part.reshape(new_shape)
    imag_view = imag_part.reshape(new_shape)
    charge = real_view[..., 0, :, :, 0, :] + real_view[..., 1, :, :, 1, :]
    moment_first = real_view[..., 0, :, :, 1, :] + real_view[..., 1, :, :, 0, :]
    moment_second = imag_view[..., 1, :, :, 0, :] - imag_view[..., 0, :, :, 1, :]
    moment_third = real_view[..., 0, :, :, 0, :] - real_view[..., 1, :, :, 1, :]
    return jnp.stack([charge, moment_first, moment_second, moment_third], axis=-4)


def reference(panels, energy_weight, block_orbitals, pattern_columns, request_source, request_local, orbital_values):
    block_width = panels.shape[3] // 2
    orbital_index = jnp.arange(2 * block_width) % block_width
    kept_mask = (orbital_index[None, :] < block_orbitals[:, None]).astype(panels.dtype)
    masked = panels * kept_mask[None, :, None, :, None]

    def one_block(block_id):
        row_panel = masked[:, block_id].astype(jnp.float32)
        column_panel = jnp.take(masked, pattern_columns[block_id].astype(jnp.int32), axis=1).astype(jnp.float32)
        left_side = jnp.stack([jnp.concatenate([row_panel[:, 0], row_panel[:, 1]], axis=-1),
                               jnp.concatenate([row_panel[:, 1], -row_panel[:, 0]], axis=-1)], axis=1)
        right_side = jnp.concatenate([column_panel[:, :, 0], column_panel[:, :, 1]], axis=-1)
        product = jnp.einsum('ecak,enbk->ecanb', left_side, right_side)
        spin_blocks = spin_parts(product[:, 0], product[:, 1])
        partial_value = (energy_weight[:, None, None, None, None] * spin_blocks).astype(jnp.bfloat16)
        partial_value = lax.optimization_barrier(partial_value).astype(jnp.float32)
        return jnp.sum(partial_value, axis=0).astype(jnp.bfloat16).reshape(4 * block_width, -1)

    density_rows = lax.map(one_block, jnp.arange(NB).astype(jnp.int32))
    device_count = N_ENERGY * N_ROWS
    sources = request_source[:, 0].reshape(device_count, REQ_DEV)
    local_ids = request_local.reshape(device_count, REQ_DEV)
    values_all = orbital_values.reshape(device_count, REQ_DEV, NNZ * block_width, CELLS_DEV)

    def one_device(pieces):
        source_ids, block_ids, values = pieces
        picked = jnp.take(density_rows, (source_ids * RB + block_ids).astype(jnp.int32), axis=0).astype(jnp.float32)
        applied = jnp.einsum('rab,rbp->rap', picked, values.astype(jnp.float32))
        applied = applied.reshape(REQ_DEV, 4, block_width, CELLS_DEV)
        orbital_rows = values[:, :block_width].astype(jnp.float32)
        return jnp.sum(orbital_rows[:, None] * applied, axis=(0, 2))

    per_device = lax.map(one_device, (sources, local_ids, values_all))
    return jnp.transpose(per_device, (1, 0, 2)).reshape(4, device_count * CELLS_DEV)
```

```python
import functools

import jax
import jax.numpy as jnp
from jax import lax
from jax.experimental import pallas as pl
from jax.experimental.pallas import tpu as pltpu
from jax.sharding import Mesh, PartitionSpec as P

NT = (((1,), (1,)), ((), ()))
TN = (((0,), (0,)), ((), ()))
VMEM_LIMIT = 56 * 1024 * 1024


def product_kernel(place, pattern, live, weight, own, prev, nxt, mine, theirs, ext, sems):
    copies = [
        pltpu.make_async_copy(src, ext.at[pl.ds(8 * n, 8)], sems.at[n])
        for n, src in enumerate((prev, own, nxt))
    ]
    for copy in copies:
        copy.start()
    for copy in copies:
        copy.wait()
    first = place[0]
    core = place[1]
    scale = weight[0]
    lane = lax.broadcasted_iota(jnp.int32, (64, 256), 1)
    row = lax.broadcasted_iota(jnp.int32, (64, 256), 0)
    half = jnp.where(lane < 128, core, 1 - core)
    orbital = half * 32 + lane % 32
    starts = (core * 32, (1 - core) * 32)

    def one(i, carry):
        def piece(part, spin, t):
            at = pl.multiple_of(spin * 64 + starts[t], 32)
            return ext[8 + i, part, pl.ds(at, 32), :]

        def stack(parts):
            return jnp.concatenate(
                [piece(part, spin, t) * sign for t in range(2) for part, spin, sign in parts], axis=0
            )

        one_ = jnp.asarray(1, jnp.bfloat16)
        neg = jnp.asarray(-1, jnp.bfloat16)
        sides = {
            (0, 0): stack([(0, 0, one_), (0, 1, one_), (0, 0, one_), (1, 1, one_)]),
            (0, 1): stack([(1, 0, one_), (1, 1, one_), (1, 0, one_), (0, 1, neg)]),
            (1, 0): stack([(0, 1, one_), (0, 0, one_), (0, 1, neg), (1, 0, neg)]),
            (1, 1): stack([(1, 1, one_), (1, 0, one_), (1, 1, neg), (0, 0, one_)]),
        }
        columns = [pattern[i, k] for k in range(6)]
        total = None
        for (spin, part), side in sides.items():
            left = jnp.concatenate(
                [ext[c - first + 8, part, pl.ds(spin * 64, 64), :] for c in columns], axis=0
            )
            term = lax.dot_general(left, side, NT, preferred_element_type=jnp.float32)
            total = term if total is None else total + term
        kept_row = orbital < live[first + i]
        pieces = []
        for k, c in enumerate(columns):
            kept = kept_row & (row < live[c])
            pieces.append(jnp.where(kept, total[64 * k : 64 * k + 64] * scale, 0.0))
        rounded = jnp.concatenate(pieces, axis=0).astype(jnp.bfloat16)
        for ref, at in ((mine, 0), (theirs, 128)):
            ref[i // 2, :, i % 2] = rounded[:, at : at + 128].reshape(8, 48, 128)
        return carry

    lax.fori_loop(0, 8, one, 0)


def products(place, pattern, live, weight, own, prev, nxt):
    smem = pl.BlockSpec(memory_space=pltpu.SMEM)
    hbm = pl.BlockSpec(memory_space=pl.ANY)
    shape = jax.ShapeDtypeStruct((4, 8, 2, 48, 128), jnp.bfloat16)
    return pl.pallas_call(
        product_kernel,
        out_shape=(shape, shape),
        in_specs=[smem] * 4 + [hbm] * 3,
        out_specs=(pl.BlockSpec(memory_space=pltpu.VMEM),) * 2,
        scratch_shapes=[
            pltpu.VMEM((24, 2, 128, 256), jnp.bfloat16),
            pltpu.SemaphoreType.DMA((3,)),
        ],
        compiler_params=pltpu.CompilerParams(vmem_limit_bytes=VMEM_LIMIT),
        cost_estimate=pl.CostEstimate(flops=1_600_000_000, bytes_accessed=5_000_000, transcendentals=0),
        name="products",
    )(place, pattern, live, weight, own, prev, nxt)


def apply_kernel(place, source, local, own_q, other_q, vals_o, *rest):
    shards, out, rows, sems = rest[:8], rest[8], rest[9], rest[10]
    z = pl.program_id(0)
    core, y_at, x_at = place[1], place[2], place[3]

    @pl.when(z == 0)
    def _():
        copies = [
            pltpu.make_async_copy(shard, rows.at[n], sems.at[n]) for n, shard in enumerate(shards)
        ]
        for copy in copies:
            copy.start()
        for copy in copies:
            copy.wait()

    for t in range(2):
        owner = jnp.where(core == 0, t, 1 - t)
        device = (2 * y_at + owner) * 32 + 4 * z + x_at
        vals_q = own_q if t == 0 else other_q

        total = jnp.zeros((4, 32, 128), jnp.float32)
        for r in range(16):
            request = device * 16 + r
            src = source[request]
            loc = local[request]
            dx = (x_at - src % 4) & 3
            dy = (y_at - loc // 2) & 3
            odd = loc % 2
            outer = jnp.where(odd == 0, dy, 4 + dx)
            inner = jnp.where(odd == 0, dx, dy)
            side = rows[outer, inner, src // 4]
            applied = lax.dot_general(side, vals_q[0, r], TN, preferred_element_type=jnp.float32)
            weights = vals_o[0, t, r].astype(jnp.float32)
            total = total + applied.reshape(4, 32, 128) * weights[None]
        sums = jnp.sum(total, axis=1)
        for at, c in enumerate((0, 1, 3, 2)):
            out[0, t, pl.ds(c, 1)] = sums[at : at + 1]


def applied_sums(place, source, local, own_q, other_q, vals_o, shards):
    smem = pl.BlockSpec(memory_space=pltpu.SMEM)
    hbm = pl.BlockSpec(memory_space=pl.ANY)
    by_z = pl.BlockSpec((1, 16, 48, 128), lambda z: (z, 0, 0, 0))
    return pl.pallas_call(
        apply_kernel,
        grid=(8,),
        out_shape=jax.ShapeDtypeStruct((8, 2, 4, 128), jnp.float32),
        in_specs=[smem] * 3
        + [by_z, by_z, pl.BlockSpec((1, 2, 16, 32, 128), lambda z: (z, 0, 0, 0, 0))]
        + [hbm] * 8,
        out_specs=pl.BlockSpec((1, 2, 4, 128), lambda z: (z, 0, 0, 0)),
        scratch_shapes=[
            pltpu.VMEM((8, 4, 8, 48, 128), jnp.bfloat16),
            pltpu.SemaphoreType.DMA((8,)),
        ],
        compiler_params=pltpu.CompilerParams(vmem_limit_bytes=VMEM_LIMIT),
        cost_estimate=pl.CostEstimate(flops=400_000_000, bytes_accessed=8_000_000, transcendentals=0),
        name="applied_sums",
    )(place, source, local, own_q, other_q, vals_o, *shards)


def shifted(value, axis, by):
    count = lax.axis_size(axis)
    return lax.ppermute(value, axis, [(n, (n + by) % count) for n in range(count)])


def gathered(value, axis):
    return [value] + [shifted(value, axis, d) for d in (1, 2, 3)]


def local_program(panels, energy_weight, block_orbitals, pattern_columns, request_source, request_local, orbital_values):
    core = lax.axis_index("core")
    y_at, z_at, x_at = lax.axis_index("y"), lax.axis_index("z"), lax.axis_index("x")
    place = jnp.stack([(z_at * 4 + x_at) * 8, core, y_at, x_at]).astype(jnp.int32)
    own = panels[0]
    forward = [(n, n + 1) for n in range(31)]
    backward = [(n + 1, n) for n in range(31)]
    swap = [(0, 1), (1, 0)]
    prev = lax.ppermute(own, ("z", "x"), forward)
    nxt = lax.ppermute(own, ("z", "x"), backward)

    values_o = orbital_values[:, :64].reshape(16, 2, 32, 128)
    keep_o = lax.dynamic_index_in_dim(values_o, core, 1, keepdims=False)
    send_o = lax.dynamic_index_in_dim(values_o, 1 - core, 1, keepdims=False)
    pair_o = jnp.stack([keep_o, lax.ppermute(send_o, "core", swap)])
    vals_o = lax.all_gather(pair_o, "z")
    chunks = orbital_values.reshape(16, 8, 48, 128).swapaxes(0, 1)
    own_q = lax.all_to_all(chunks, "z", 0, 0, tiled=True)
    other_q = lax.ppermute(own_q, "core", swap)

    mine, theirs = products(place, pattern_columns, block_orbitals, energy_weight, own, prev, nxt)
    got = lax.ppermute(theirs, "core", swap)
    pair = (mine.astype(jnp.float32) + got.astype(jnp.float32)).astype(jnp.bfloat16)
    parts = lax.all_to_all(pair.reshape(32, 2, 48, 128), ("y", "z"), 0, 0, tiled=True)
    rows = jnp.sum(parts.reshape(4, 8, 2, 48, 128).astype(jnp.float32), axis=0).astype(jnp.bfloat16)
    even = jnp.stack(gathered(rows[:, 0], "x"))
    odd = jnp.stack(gathered(rows[:, 1], "y"))
    shards = gathered(even, "y") + gathered(odd, "x")

    sums = applied_sums(place, request_source.reshape(-1), request_local, own_q, other_q, vals_o, shards)
    back = lax.ppermute(sums[:, 1], "core", swap)
    total = sums[:, 0] + back
    landed = lax.all_to_all(total, "z", 0, 0, tiled=True)
    return jnp.sum(landed, axis=0)


def solution(mesh):
    fine = Mesh(mesh.devices.reshape(4, 2, 8, 4), ("y", "core", "z", "x"))
    energy, rows = ("y", "core"), ("z", "x")
    in_specs = (
        P(energy, rows, None, None, None),
        P(energy),
        P(),
        P(rows, None),
        P(),
        P(),
        P(energy + rows, None, None),
    )
    return jax.shard_map(
        local_program, mesh=fine, in_specs=in_specs, out_specs=P(None, energy + rows), check_vma=False
    )
```

```python
import jax
import jax.numpy as jnp
from jax import lax
from jax.experimental import pallas as pl
from jax.experimental.pallas import tpu as pltpu
from jax.sharding import Mesh, PartitionSpec as P

NT = (((1,), (1,)), ((), ()))
TN = (((0,), (0,)), ((), ()))
MIB = 1024 * 1024
SMEM = pl.BlockSpec(memory_space=pltpu.SMEM)
VMEM = pl.BlockSpec(memory_space=pltpu.VMEM)
ANY = pl.BlockSpec(memory_space=pl.ANY)


def bf16(*shape):
    return jax.ShapeDtypeStruct(shape, jnp.bfloat16)


def params(mib):
    return pltpu.CompilerParams(vmem_limit_bytes=mib * MIB)


def prepare_kernel(own, sides):
    table = (
        ((0, 0, 1), (0, 1, 1), (0, 0, 1), (1, 1, 1)),
        ((1, 0, 1), (1, 1, 1), (1, 0, 1), (0, 1, -1)),
        ((0, 1, 1), (0, 0, 1), (0, 1, -1), (1, 0, -1)),
        ((1, 1, 1), (1, 0, 1), (1, 1, -1), (0, 0, 1)),
    )

    def one(i, carry):
        pieces = {(part, spin): own[i, part, pl.ds(64 * spin, 64), :] for part in range(2) for spin in range(2)}
        for n, parts in enumerate(table):
            for c, (part, spin, sign) in enumerate(parts):
                piece = pieces[part, spin]
                sides[i, n, pl.ds(64 * c, 64), :] = piece if sign == 1 else -piece
        return carry

    lax.fori_loop(0, 8, one, 0)


def prepare(own):
    return pl.pallas_call(
        prepare_kernel,
        out_shape=bf16(8, 4, 256, 256),
        in_specs=[VMEM],
        out_specs=VMEM,
        compiler_params=params(10),
        cost_estimate=pl.CostEstimate(flops=0, bytes_accessed=5_000_000, transcendentals=0),
        name="prepare",
    )(own)


def cut_kernel(values, chunks, orbitals):
    for e in range(8):
        chunks[e] = values[:, pl.ds(48 * e, 48)]
    orbitals[...] = values[:, :64]


def cut_values(values):
    return pl.pallas_call(
        cut_kernel,
        out_shape=(bf16(8, 16, 48, 128), bf16(16, 64, 128)),
        in_specs=[VMEM],
        out_specs=(VMEM, VMEM),
        compiler_params=params(8),
        cost_estimate=pl.CostEstimate(flops=0, bytes_accessed=3_000_000, transcendentals=0),
        name="cut_values",
    )(values)


def gate_kernel(*refs):
    pass


def gate(value, *after):
    return pl.pallas_call(
        gate_kernel,
        out_shape=jax.ShapeDtypeStruct(value.shape, value.dtype),
        in_specs=[ANY] * (1 + len(after)),
        out_specs=ANY,
        input_output_aliases={0: 0},
        compiler_params=params(1),
        cost_estimate=pl.CostEstimate(flops=0, bytes_accessed=0, transcendentals=0),
        name="gate",
    )(value, *after)


def product_kernel(place, pattern, live, weight, sides, low, own, high, mine, theirs, ext, sems):
    i = pl.program_id(0)

    @pl.when(i == 0)
    def _():
        copies = [
            pltpu.make_async_copy(src, ext.at[pl.ds(8 * n, 8)], sems.at[n]) for n, src in enumerate((low, own, high))
        ]
        for copy in copies:
            copy.start()
        for copy in copies:
            copy.wait()

    first = place[0]
    scale = weight[0]
    even = place[1] == 0
    orbital = lax.broadcasted_iota(jnp.int32, (64, 256), 1) % 64
    row = lax.broadcasted_iota(jnp.int32, (64, 256), 0)
    columns = [pattern[i, k] for k in range(6)]
    total = None
    for n, (spin, part) in enumerate(((0, 0), (0, 1), (1, 0), (1, 1))):
        left = jnp.concatenate([ext[c - first + 8, part, pl.ds(spin * 64, 64), :] for c in columns], axis=0)
        term = lax.dot_general(left, sides[0, n], NT, preferred_element_type=jnp.float32)
        total = term if total is None else total + term
    kept_row = orbital < live[first + i]
    pieces = []
    for k, c in enumerate(columns):
        kept = kept_row & (row < live[c])
        pieces.append(jnp.where(kept, total[64 * k : 64 * k + 64] * scale, 0.0))
    chunks = jnp.concatenate(pieces, axis=0).reshape(4, 2, 48, 256)
    mine[:, 0] = jnp.where(even, chunks[:, 0], chunks[:, 1]).astype(jnp.bfloat16)
    theirs[:, 0] = jnp.where(even, chunks[:, 1], chunks[:, 0]).astype(jnp.bfloat16)


def products(place, pattern, live, weight, sides, low, own, high):
    by_block = pl.BlockSpec((4, 1, 48, 256), lambda i: (0, i, 0, 0))
    return pl.pallas_call(
        product_kernel,
        grid=(8,),
        out_shape=(bf16(4, 8, 48, 256),) * 2,
        in_specs=[SMEM] * 4 + [pl.BlockSpec((1, 4, 256, 256), lambda i: (i, 0, 0, 0))] + [ANY] * 3,
        out_specs=(by_block, by_block),
        scratch_shapes=[pltpu.VMEM((24, 2, 128, 256), jnp.bfloat16), pltpu.SemaphoreType.DMA((3,))],
        compiler_params=params(12),
        cost_estimate=pl.CostEstimate(flops=1_600_000_000, bytes_accessed=9_000_000, transcendentals=0),
        name="products",
    )(place, pattern, live, weight, sides, low, own, high)


def pair_kernel(place, mine, got, *parts):
    for d in range(4):
        at = (place[2] + d) & 3
        parts[d][...] = (mine[at].astype(jnp.float32) + got[at].astype(jnp.float32)).astype(jnp.bfloat16)


def pair_sums(place, mine, got):
    return pl.pallas_call(
        pair_kernel,
        out_shape=(bf16(8, 48, 256),) * 4,
        in_specs=[SMEM, VMEM, VMEM],
        out_specs=(VMEM,) * 4,
        compiler_params=params(6),
        cost_estimate=pl.CostEstimate(flops=400_000, bytes_accessed=2_400_000, transcendentals=0),
        name="pair_sums",
    )(place, mine, got)


def apply_kernel(place, source, local, vals_q, own_o, other_o, *rest):
    count = len(rest) - 3
    shards, out, rows, sems = rest[:count], rest[count], rest[count + 1], rest[count + 2]
    e = pl.program_id(0)
    core, y_at, x_at, z_at = place[1], place[2], place[3], place[4]

    @pl.when(e == 0)
    def _():
        at, copies = 0, []
        for n, shard in enumerate(shards):
            size = shard.shape[0]
            copies.append(pltpu.make_async_copy(shard, rows.at[pl.ds(at, size)], sems.at[n]))
            at += size
        for copy in copies:
            copy.start()
        for copy in copies:
            copy.wait()

    device = e * 32 + 4 * z_at + x_at
    dy = (y_at - e // 2) & 3
    same = (e & 1) == core

    def run(values_o):
        total = jnp.zeros((4, 64, 128), jnp.float32)
        for r in range(16):
            request = device * 16 + r
            src = source[request]
            loc = local[request]
            dx = (x_at - src) & 3
            dz = (z_at - src // 4) & 7
            at = jnp.where(loc < 4, 16 * dz + 4 * dx + loc, 128 + 32 * dx + 4 * dz + loc - 4)
            applied = lax.dot_general(rows[at], vals_q[0, r], TN, preferred_element_type=jnp.float32)
            total = total + applied.reshape(4, 64, 128) * values_o[dy, r].astype(jnp.float32)[None]
        sums = jnp.sum(total, axis=1)
        for at, c in enumerate((0, 1, 3, 2)):
            out[0, pl.ds(c, 1)] = sums[at : at + 1]

    @pl.when(same)
    def _():
        run(own_o)

    @pl.when(jnp.logical_not(same))
    def _():
        run(other_o)


def applied_sums(place, source, local, vals_q, own_o, other_o, shards):
    return pl.pallas_call(
        apply_kernel,
        grid=(8,),
        out_shape=jax.ShapeDtypeStruct((8, 4, 128), jnp.float32),
        in_specs=[SMEM] * 3
        + [pl.BlockSpec((1, 16, 48, 128), lambda e: (e, 0, 0, 0)), VMEM, VMEM]
        + [ANY] * len(shards),
        out_specs=pl.BlockSpec((1, 4, 128), lambda e: (e, 0, 0)),
        scratch_shapes=[pltpu.VMEM((256, 48, 256), jnp.bfloat16), pltpu.SemaphoreType.DMA((len(shards),))],
        compiler_params=params(56),
        cost_estimate=pl.CostEstimate(flops=400_000_000, bytes_accessed=8_000_000, transcendentals=0),
        name="applied_sums",
    )(place, source, local, vals_q, own_o, other_o, *shards)


def shifted(value, axis, by):
    count = lax.axis_size(axis)
    return lax.ppermute(value, axis, [(n, (n + by) % count) for n in range(count)])


def gathered(value, axis):
    return [value] + [shifted(value, axis, d) for d in (1, 2, 3)]


def three_ways(value):
    ahead, behind, around = value, value, {0: value}
    for step in (1, 2, 3):
        ahead, behind = shifted(ahead, "z", 1), shifted(behind, "z", 7)
        around[step], around[8 - step] = ahead, behind
    return around, ahead, behind


def flat(value):
    return value.reshape((-1,) + value.shape[-2:])


def local_program(panels, energy_weight, block_orbitals, pattern_columns, request_source, request_local, orbital_values):
    core = lax.axis_index("core")
    y_at, z_at, x_at = lax.axis_index("y"), lax.axis_index("z"), lax.axis_index("x")
    place = jnp.stack([(z_at * 4 + x_at) * 8, core, y_at, x_at, z_at]).astype(jnp.int32)
    own = panels[0]
    swap = [(0, 1), (1, 0)]
    low = lax.ppermute(own, ("z", "x"), [(n, n + 1) for n in range(31)])
    high = lax.ppermute(own, ("z", "x"), [(n + 1, n) for n in range(31)])

    chunks, orbitals = cut_values(orbital_values)
    own_o = jnp.stack(gathered(orbitals, "y"))
    other_o = lax.ppermute(own_o, "core", swap)
    vals_q = lax.all_to_all(chunks, ("y", "core"), 0, 0, tiled=True)
    sides = gate(prepare(own), vals_q, own_o)

    mine, theirs = products(place, pattern_columns, block_orbitals, energy_weight, sides, low, own, high)
    got = lax.ppermute(theirs, "core", swap)
    parts = pair_sums(place, mine, got)
    total = parts[0].astype(jnp.float32)
    for d in (1, 2, 3):
        total = total + shifted(parts[d], "y", d).astype(jnp.float32)
    total = total.astype(jnp.bfloat16)

    first = jnp.stack(gathered(total[:4], "x"))
    firsts, ahead, behind = three_ways(first)
    last = [shifted(ahead[:2], "z", 1), shifted(behind[2:], "z", 7)]
    shards = [firsts[d] for d in range(4)] + last + [firsts[d] for d in (5, 6, 7)]
    seconds, ahead, behind = three_ways(total[4:])
    seconds[4] = shifted(ahead, "z", 1)
    second = jnp.stack([seconds[d] for d in range(8)])
    right, left = shifted(second, "x", 1), shifted(second, "x", 3)
    shards += [second, right, shifted(right[:4], "x", 1), shifted(left[4:], "x", 3), left]

    sums = applied_sums(
        place, request_source.reshape(-1), request_local, vals_q, own_o, other_o, [flat(s) for s in shards]
    )
    landed = lax.all_to_all(sums, ("y", "core"), 0, 0, tiled=True)
    return jnp.sum(landed, axis=0)


def solution(mesh):
    fine = Mesh(mesh.devices.reshape(4, 2, 8, 4), ("y", "core", "z", "x"))
    energy, rows = ("y", "core"), ("z", "x")
    in_specs = (
        P(energy, rows, None, None, None),
        P(energy),
        P(),
        P(rows, None),
        P(),
        P(),
        P(energy + rows, None, None),
    )
    return jax.shard_map(
        local_program, mesh=fine, in_specs=in_specs, out_specs=P(None, energy + rows), check_vma=False
    )
```

```python
import jax
import jax.numpy as jnp
from jax import lax
from jax.experimental import pallas as pl
from jax.experimental.pallas import tpu as pltpu
from jax.sharding import Mesh, PartitionSpec as P

NT = (((1,), (1,)), ((), ()))
TN = (((0,), (0,)), ((), ()))
MIB = 1024 * 1024
SMEM = pl.BlockSpec(memory_space=pltpu.SMEM)
VMEM = pl.BlockSpec(memory_space=pltpu.VMEM)
ANY = pl.BlockSpec(memory_space=pl.ANY)
SPLIT = 5


def bf16(*shape):
    return jax.ShapeDtypeStruct(shape, jnp.bfloat16)


def params(mib):
    return pltpu.CompilerParams(vmem_limit_bytes=mib * MIB)


def prepare_kernel(own, sides):
    table = (
        ((0, 0, 1), (0, 1, 1), (0, 0, 1), (1, 1, 1)),
        ((1, 0, 1), (1, 1, 1), (1, 0, 1), (0, 1, -1)),
        ((0, 1, 1), (0, 0, 1), (0, 1, -1), (1, 0, -1)),
        ((1, 1, 1), (1, 0, 1), (1, 1, -1), (0, 0, 1)),
    )

    def one(i, carry):
        pieces = {(part, spin): own[i, part, pl.ds(64 * spin, 64), :] for part in range(2) for spin in range(2)}
        for n, parts in enumerate(table):
            for c, (part, spin, sign) in enumerate(parts):
                piece = pieces[part, spin]
                sides[i, n, pl.ds(64 * c, 64), :] = piece if sign == 1 else -piece
        return carry

    lax.fori_loop(0, 8, one, 0)


def prepare(own):
    return pl.pallas_call(
        prepare_kernel,
        out_shape=bf16(8, 4, 256, 256),
        in_specs=[VMEM],
        out_specs=VMEM,
        compiler_params=params(10),
        cost_estimate=pl.CostEstimate(flops=0, bytes_accessed=5_000_000, transcendentals=0),
        name="prepare",
    )(own)


def cut_kernel(values, chunks, orbitals):
    for e in range(8):
        chunks[e] = values[:, pl.ds(48 * e, 48)]
    orbitals[...] = values[:, :64]


def cut_values(values):
    return pl.pallas_call(
        cut_kernel,
        out_shape=(bf16(8, 16, 48, 128), bf16(16, 64, 128)),
        in_specs=[VMEM],
        out_specs=(VMEM, VMEM),
        compiler_params=params(8),
        cost_estimate=pl.CostEstimate(flops=0, bytes_accessed=3_000_000, transcendentals=0),
        name="cut_values",
    )(values)


def product_kernel(place, pattern, live, weight, sides, low, own, high, mine, theirs, ext, sems):
    i = pl.program_id(0)

    @pl.when(i == 0)
    def _():
        copies = [
            pltpu.make_async_copy(src, ext.at[pl.ds(8 * n, 8)], sems.at[n]) for n, src in enumerate((low, own, high))
        ]
        for copy in copies:
            copy.start()
        for copy in copies:
            copy.wait()

    first = place[0]
    scale = weight[0]
    even = place[1] == 0
    orbital = lax.broadcasted_iota(jnp.int32, (64, 256), 1) % 64
    row = lax.broadcasted_iota(jnp.int32, (64, 256), 0)
    columns = [pattern[i, k] for k in range(6)]
    total = None
    for n, (spin, part) in enumerate(((0, 0), (0, 1), (1, 0), (1, 1))):
        left = jnp.concatenate([ext[c - first + 8, part, pl.ds(spin * 64, 64), :] for c in columns], axis=0)
        term = lax.dot_general(left, sides[0, n], NT, preferred_element_type=jnp.float32)
        total = term if total is None else total + term
    kept_row = orbital < live[first + i]
    pieces = []
    for k, c in enumerate(columns):
        kept = kept_row & (row < live[c])
        pieces.append(jnp.where(kept, total[64 * k : 64 * k + 64] * scale, 0.0))
    chunks = jnp.concatenate(pieces, axis=0).reshape(4, 2, 48, 256)
    mine[:, 0] = jnp.where(even, chunks[:, 0], chunks[:, 1]).astype(jnp.bfloat16)
    theirs[:, 0] = jnp.where(even, chunks[:, 1], chunks[:, 0]).astype(jnp.bfloat16)


def products(place, pattern, live, weight, sides, low, own, high):
    by_block = pl.BlockSpec((4, 1, 48, 256), lambda i: (0, i, 0, 0))
    return pl.pallas_call(
        product_kernel,
        grid=(8,),
        out_shape=(bf16(4, 8, 48, 256),) * 2,
        in_specs=[SMEM] * 4 + [pl.BlockSpec((1, 4, 256, 256), lambda i: (i, 0, 0, 0))] + [ANY] * 3,
        out_specs=(by_block, by_block),
        scratch_shapes=[pltpu.VMEM((24, 2, 128, 256), jnp.bfloat16), pltpu.SemaphoreType.DMA((3,))],
        compiler_params=params(12),
        cost_estimate=pl.CostEstimate(flops=1_600_000_000, bytes_accessed=9_000_000, transcendentals=0),
        name="products",
    )(place, pattern, live, weight, sides, low, own, high)


def pair_kernel(place, landed, mine, got, *parts):
    for d in range(4):
        at = (place[2] + d) & 3
        parts[d][...] = (mine[at].astype(jnp.float32) + got[at].astype(jnp.float32)).astype(jnp.bfloat16)


def pair_sums(place, landed, mine, got):
    return pl.pallas_call(
        pair_kernel,
        out_shape=(bf16(8, 48, 256),) * 4,
        in_specs=[SMEM, ANY, VMEM, VMEM],
        out_specs=(VMEM,) * 4,
        compiler_params=params(6),
        cost_estimate=pl.CostEstimate(flops=400_000, bytes_accessed=2_400_000, transcendentals=0),
        name="pair_sums",
    )(place, landed, mine, got)


def apply_kernel(place, source, local, vals_q, own_o, other_o, *rest):
    count = len(rest) - 3
    shards, out, rows, sems = rest[:count], rest[count], rest[count + 1], rest[count + 2]
    e = pl.program_id(0)
    core, y_at, x_at, z_at = place[1], place[2], place[3], place[4]

    @pl.when(e == 0)
    def _():
        at, copies = 0, []
        for n, shard in enumerate(shards):
            size = shard.shape[0]
            copies.append(pltpu.make_async_copy(shard, rows.at[pl.ds(at, size)], sems.at[n]))
            at += size
        for copy in copies:
            copy.start()
        for copy in copies:
            copy.wait()

    device = e * 32 + 4 * z_at + x_at
    dy = (y_at - e // 2) & 3
    same = (e & 1) == core

    def run(values_o):
        total = jnp.zeros((4, 8, 128), jnp.float32)
        for r in range(16):
            request = device * 16 + r
            src = source[request]
            loc = local[request]
            dx = (x_at - src) & 3
            dz = (z_at - src // 4) & 7
            at = jnp.where(
                loc < SPLIT,
                SPLIT * (4 * dz + dx) + loc,
                32 * SPLIT + (8 - SPLIT) * (8 * dx + dz) + loc - SPLIT,
            )
            applied = lax.dot_general(rows[at], vals_q[0, r], TN, preferred_element_type=jnp.float32)
            weighted = applied.reshape(4, 8, 8, 128) * values_o[dy, r].astype(jnp.float32).reshape(1, 8, 8, 128)
            total = total + jnp.sum(weighted, axis=1)
        sums = jnp.sum(total, axis=1)
        for at, c in enumerate((0, 1, 3, 2)):
            out[0, pl.ds(c, 1)] = sums[at : at + 1]

    @pl.when(same)
    def _():
        run(own_o)

    @pl.when(jnp.logical_not(same))
    def _():
        run(other_o)


def applied_sums(place, source, local, vals_q, own_o, other_o, shards):
    return pl.pallas_call(
        apply_kernel,
        grid=(8,),
        out_shape=jax.ShapeDtypeStruct((8, 4, 128), jnp.float32),
        in_specs=[SMEM] * 3
        + [pl.BlockSpec((1, 16, 48, 128), lambda e: (e, 0, 0, 0)), VMEM, VMEM]
        + [ANY] * len(shards),
        out_specs=pl.BlockSpec((1, 4, 128), lambda e: (e, 0, 0)),
        scratch_shapes=[pltpu.VMEM((256, 48, 256), jnp.bfloat16), pltpu.SemaphoreType.DMA((len(shards),))],
        compiler_params=params(56),
        cost_estimate=pl.CostEstimate(flops=400_000_000, bytes_accessed=8_000_000, transcendentals=0),
        name="applied_sums",
    )(place, source, local, vals_q, own_o, other_o, *shards)


def shifted(value, axis, by):
    count = lax.axis_size(axis)
    return lax.ppermute(value, axis, [(n, (n + by) % count) for n in range(count)])


def gathered(value, axis):
    return [value] + [shifted(value, axis, d) for d in (1, 2, 3)]


def three_ways(value):
    ahead, behind, around = value, value, {0: value}
    for step in (1, 2, 3):
        ahead, behind = shifted(ahead, "z", 1), shifted(behind, "z", 7)
        around[step], around[8 - step] = ahead, behind
    return around, ahead, behind


def flat(value):
    return value.reshape((-1,) + value.shape[-2:])


def local_program(panels, energy_weight, block_orbitals, pattern_columns, request_source, request_local, orbital_values):
    core = lax.axis_index("core")
    y_at, z_at, x_at = lax.axis_index("y"), lax.axis_index("z"), lax.axis_index("x")
    place = jnp.stack([(z_at * 4 + x_at) * 8, core, y_at, x_at, z_at]).astype(jnp.int32)
    own = panels[0]
    swap = [(0, 1), (1, 0)]
    low = lax.ppermute(own, ("z", "x"), [(n, n + 1) for n in range(31)])
    high = lax.ppermute(own, ("z", "x"), [(n + 1, n) for n in range(31)])

    chunks, orbitals = cut_values(orbital_values)
    own_o = jnp.stack(gathered(orbitals, "y"))
    other_o = lax.ppermute(own_o, "core", swap)
    vals_q = lax.all_to_all(chunks, ("y", "core"), 0, 0, tiled=True)
    sides = prepare(own)
    landed = jnp.stack([vals_q[0, 0, :8], own_o[1, 0, :8] + own_o[2, 0, :8] + own_o[3, 0, :8]])

    mine, theirs = products(place, pattern_columns, block_orbitals, energy_weight, sides, low, own, high)
    got = lax.ppermute(theirs, "core", swap)
    parts = pair_sums(place, landed, mine, got)
    total = parts[0].astype(jnp.float32)
    for d in (1, 2, 3):
        total = total + shifted(parts[d], "y", d).astype(jnp.float32)
    total = total.astype(jnp.bfloat16)

    seconds, ahead, behind = three_ways(total[SPLIT:])
    seconds[4] = shifted(ahead, "z", 1)
    over_x = gathered(total[:SPLIT], "x")
    first = jnp.stack(over_x)
    second = jnp.stack([seconds[d] for d in range(8)])
    firsts, ahead, behind = three_ways(first)
    last = [shifted(ahead[:2], "z", 1), shifted(behind[2:], "z", 7)]
    shards = [firsts[d] for d in range(4)] + last + [firsts[d] for d in (5, 6, 7)]
    right, left = shifted(second, "x", 1), shifted(second, "x", 3)
    shards += [second, right, shifted(right[:4], "x", 1), shifted(left[4:], "x", 3), left]

    sums = applied_sums(
        place, request_source.reshape(-1), request_local, vals_q, own_o, other_o, [flat(s) for s in shards]
    )
    return jnp.sum(lax.all_to_all(sums, ("y", "core"), 0, 0, tiled=True), axis=0)


def solution(mesh):
    fine = Mesh(mesh.devices.reshape(4, 2, 8, 4), ("y", "core", "z", "x"))
    energy, rows = ("y", "core"), ("z", "x")
    in_specs = (
        P(energy, rows, None, None, None),
        P(energy),
        P(),
        P(rows, None),
        P(),
        P(),
        P(energy + rows, None, None),
    )
    return jax.shard_map(
        local_program, mesh=fine, in_specs=in_specs, out_specs=P(None, energy + rows), check_vma=False
    )
```

```python
import jax
import jax.numpy as jnp
from jax import lax
from jax.experimental import pallas as pl
from jax.experimental.pallas import tpu as pltpu
from jax.sharding import Mesh, PartitionSpec as P

NT = (((1,), (1,)), ((), ()))
TN = (((0,), (0,)), ((), ()))
MIB = 1024 * 1024
SMEM = pl.BlockSpec(memory_space=pltpu.SMEM)
VMEM = pl.BlockSpec(memory_space=pltpu.VMEM)
ANY = pl.BlockSpec(memory_space=pl.ANY)
SPLIT = 5


def bf16(*shape):
    return jax.ShapeDtypeStruct(shape, jnp.bfloat16)


def params(mib):
    return pltpu.CompilerParams(vmem_limit_bytes=mib * MIB)


SIDES = {
    (0, 0): ((0, 0, 1), (0, 1, 1), (0, 0, 1), (1, 1, 1)),
    (0, 1): ((1, 0, 1), (1, 1, 1), (1, 0, 1), (0, 1, -1)),
    (1, 0): ((0, 1, 1), (0, 0, 1), (0, 1, -1), (1, 0, -1)),
    (1, 1): ((1, 1, 1), (1, 0, 1), (1, 1, -1), (0, 0, 1)),
}


def cut_kernel(values, chunks, orbitals):
    for e in range(8):
        chunks[e] = values[:, pl.ds(48 * e, 48)]
    orbitals[...] = values[:, :64]


def cut_values(values):
    return pl.pallas_call(
        cut_kernel,
        out_shape=(bf16(8, 16, 48, 128), bf16(16, 64, 128)),
        in_specs=[VMEM],
        out_specs=(VMEM, VMEM),
        compiler_params=params(8),
        cost_estimate=pl.CostEstimate(flops=0, bytes_accessed=3_000_000, transcendentals=0),
        name="cut_values",
    )(values)


def product_kernel(place, pattern, live, weight, low, own, high, mine, theirs, ext, sems):
    i = pl.program_id(0)

    @pl.when(i == 0)
    def _():
        copies = [
            pltpu.make_async_copy(src, ext.at[pl.ds(8 * n, 8)], sems.at[n]) for n, src in enumerate((low, own, high))
        ]
        for copy in copies:
            copy.start()
        for copy in copies:
            copy.wait()

    first = place[0]
    scale = weight[0]
    even = place[1] == 0
    orbital = lax.broadcasted_iota(jnp.int32, (64, 256), 1) % 64
    row = lax.broadcasted_iota(jnp.int32, (64, 256), 0)
    columns = [pattern[i, k] for k in range(6)]
    total = None
    own_pieces = {(part, spin): ext[8 + i, part, pl.ds(64 * spin, 64), :] for part in range(2) for spin in range(2)}
    for (spin, part), rows in SIDES.items():
        side = jnp.concatenate([own_pieces[p, s] if sign == 1 else -own_pieces[p, s] for p, s, sign in rows], axis=0)
        left = jnp.concatenate([ext[c - first + 8, part, pl.ds(spin * 64, 64), :] for c in columns], axis=0)
        term = lax.dot_general(left, side, NT, preferred_element_type=jnp.float32)
        total = term if total is None else total + term
    kept_row = orbital < live[first + i]
    pieces = []
    for k, c in enumerate(columns):
        kept = kept_row & (row < live[c])
        pieces.append(jnp.where(kept, total[64 * k : 64 * k + 64] * scale, 0.0))
    chunks = jnp.concatenate(pieces, axis=0).reshape(4, 2, 48, 256)
    mine[:, 0] = jnp.where(even, chunks[:, 0], chunks[:, 1]).astype(jnp.bfloat16)
    theirs[:, 0] = jnp.where(even, chunks[:, 1], chunks[:, 0]).astype(jnp.bfloat16)


def products(place, pattern, live, weight, low, own, high):
    by_block = pl.BlockSpec((4, 1, 48, 256), lambda i: (0, i, 0, 0))
    return pl.pallas_call(
        product_kernel,
        grid=(8,),
        out_shape=(bf16(4, 8, 48, 256),) * 2,
        in_specs=[SMEM] * 4 + [ANY] * 3,
        out_specs=(by_block, by_block),
        scratch_shapes=[pltpu.VMEM((24, 2, 128, 256), jnp.bfloat16), pltpu.SemaphoreType.DMA((3,))],
        compiler_params=params(12),
        cost_estimate=pl.CostEstimate(flops=1_600_000_000, bytes_accessed=9_000_000, transcendentals=0),
        name="products",
    )(place, pattern, live, weight, low, own, high)


def pair_kernel(place, landed, mine, got, *parts):
    for d in range(4):
        at = (place[2] + d) & 3
        parts[d][...] = (mine[at].astype(jnp.float32) + got[at].astype(jnp.float32)).astype(jnp.bfloat16)


def pair_sums(place, landed, mine, got):
    return pl.pallas_call(
        pair_kernel,
        out_shape=(bf16(8, 48, 256),) * 4,
        in_specs=[SMEM, ANY, VMEM, VMEM],
        out_specs=(VMEM,) * 4,
        compiler_params=params(6),
        cost_estimate=pl.CostEstimate(flops=400_000, bytes_accessed=2_400_000, transcendentals=0),
        name="pair_sums",
    )(place, landed, mine, got)


def apply_kernel(place, source, local, vals_q, own_o, other_o, *rest):
    count = len(rest) - 3
    shards, out, rows, sems = rest[:count], rest[count], rest[count + 1], rest[count + 2]
    e = pl.program_id(0)
    core, y_at, x_at, z_at = place[1], place[2], place[3], place[4]

    @pl.when(e == 0)
    def _():
        at, copies = 0, []
        for n, shard in enumerate(shards):
            size = shard.shape[0]
            copies.append(pltpu.make_async_copy(shard, rows.at[pl.ds(at, size)], sems.at[n]))
            at += size
        for copy in copies:
            copy.start()
        for copy in copies:
            copy.wait()

    device = e * 32 + 4 * z_at + x_at
    dy = (y_at - e // 2) & 3
    same = (e & 1) == core

    def run(values_o):
        total = jnp.zeros((4, 8, 128), jnp.float32)
        for r in range(16):
            request = device * 16 + r
            src = source[request]
            loc = local[request]
            dx = (x_at - src) & 3
            dz = (z_at - src // 4) & 7
            at = jnp.where(
                loc < SPLIT,
                SPLIT * (4 * dz + dx) + loc,
                32 * SPLIT + (8 - SPLIT) * (8 * dx + dz) + loc - SPLIT,
            )
            applied = lax.dot_general(rows[at], vals_q[0, r], TN, preferred_element_type=jnp.float32)
            weighted = applied.reshape(4, 8, 8, 128) * values_o[dy, r].astype(jnp.float32).reshape(1, 8, 8, 128)
            total = total + jnp.sum(weighted, axis=1)
        sums = jnp.sum(total, axis=1)
        for at, c in enumerate((0, 1, 3, 2)):
            out[0, pl.ds(c, 1)] = sums[at : at + 1]

    @pl.when(same)
    def _():
        run(own_o)

    @pl.when(jnp.logical_not(same))
    def _():
        run(other_o)


def applied_sums(place, source, local, vals_q, own_o, other_o, shards):
    return pl.pallas_call(
        apply_kernel,
        grid=(8,),
        out_shape=jax.ShapeDtypeStruct((8, 4, 128), jnp.float32),
        in_specs=[SMEM] * 3
        + [pl.BlockSpec((1, 16, 48, 128), lambda e: (e, 0, 0, 0)), VMEM, VMEM]
        + [ANY] * len(shards),
        out_specs=pl.BlockSpec((1, 4, 128), lambda e: (e, 0, 0)),
        scratch_shapes=[pltpu.VMEM((256, 48, 256), jnp.bfloat16), pltpu.SemaphoreType.DMA((len(shards),))],
        compiler_params=params(24),
        cost_estimate=pl.CostEstimate(flops=400_000_000, bytes_accessed=8_000_000, transcendentals=0),
        name="applied_sums",
    )(place, source, local, vals_q, own_o, other_o, *shards)


def shifted(value, axis, by):
    count = lax.axis_size(axis)
    return lax.ppermute(value, axis, [(n, (n + by) % count) for n in range(count)])


def gathered(value, axis):
    return [value] + [shifted(value, axis, d) for d in (1, 2, 3)]


def three_ways(value):
    ahead, behind, around = value, value, {0: value}
    for step in (1, 2, 3):
        ahead, behind = shifted(ahead, "z", 1), shifted(behind, "z", 7)
        around[step], around[8 - step] = ahead, behind
    return around, ahead, behind


def flat(value):
    return value.reshape((-1,) + value.shape[-2:])


def local_program(panels, energy_weight, block_orbitals, pattern_columns, request_source, request_local, orbital_values):
    core = lax.axis_index("core")
    y_at, z_at, x_at = lax.axis_index("y"), lax.axis_index("z"), lax.axis_index("x")
    place = jnp.stack([(z_at * 4 + x_at) * 8, core, y_at, x_at, z_at]).astype(jnp.int32)
    own = panels[0]
    swap = [(0, 1), (1, 0)]
    low = lax.ppermute(own, ("z", "x"), [(n, n + 1) for n in range(31)])
    high = lax.ppermute(own, ("z", "x"), [(n + 1, n) for n in range(31)])

    chunks, orbitals = cut_values(orbital_values)
    own_o = jnp.stack(gathered(orbitals, "y"))
    other_o = lax.ppermute(own_o, "core", swap)
    vals_q = lax.all_to_all(chunks, ("y", "core"), 0, 0, tiled=True)
    landed = jnp.stack([vals_q[0, 0, :8], own_o[1, 0, :8] + own_o[2, 0, :8] + own_o[3, 0, :8]])

    mine, theirs = products(place, pattern_columns, block_orbitals, energy_weight, low, own, high)
    got = lax.ppermute(theirs, "core", swap)
    parts = pair_sums(place, landed, mine, got)
    total = parts[0].astype(jnp.float32)
    for d in (1, 2, 3):
        total = total + shifted(parts[d], "y", d).astype(jnp.float32)
    total = total.astype(jnp.bfloat16)

    seconds, ahead, behind = three_ways(total[SPLIT:])
    seconds[4] = shifted(ahead, "z", 1)
    over_x = gathered(total[:SPLIT], "x")
    first = jnp.stack(over_x)
    second = jnp.stack([seconds[d] for d in range(8)])
    firsts, ahead, behind = three_ways(first)
    last = [shifted(ahead[:2], "z", 1), shifted(behind[2:], "z", 7)]
    shards = [firsts[d] for d in range(4)] + last + [firsts[d] for d in (5, 6, 7)]
    right, left = shifted(second, "x", 1), shifted(second, "x", 3)
    shards += [second, right, shifted(right[:4], "x", 1), shifted(left[4:], "x", 3), left]

    sums = applied_sums(
        place, request_source.reshape(-1), request_local, vals_q, own_o, other_o, [flat(s) for s in shards]
    )
    return jnp.sum(lax.all_to_all(sums, ("y", "core"), 0, 0, tiled=True), axis=0)


def solution(mesh):
    fine = Mesh(mesh.devices.reshape(4, 2, 8, 4), ("y", "core", "z", "x"))
    energy, rows = ("y", "core"), ("z", "x")
    in_specs = (
        P(energy, rows, None, None, None),
        P(energy),
        P(),
        P(rows, None),
        P(),
        P(),
        P(energy + rows, None, None),
    )
    return jax.shard_map(
        local_program, mesh=fine, in_specs=in_specs, out_specs=P(None, energy + rows), check_vma=False
    )
```

```python
import jax
import jax.numpy as jnp
from jax import lax
from jax.experimental import pallas as pl
from jax.experimental.pallas import tpu as pltpu
from jax.sharding import Mesh, PartitionSpec as P

NT = (((1,), (1,)), ((), ()))
TN = (((0,), (0,)), ((), ()))
MIB = 1024 * 1024
SMEM = pl.BlockSpec(memory_space=pltpu.SMEM)
VMEM = pl.BlockSpec(memory_space=pltpu.VMEM)
ANY = pl.BlockSpec(memory_space=pl.ANY)
SPLIT = 5


def bf16(*shape):
    return jax.ShapeDtypeStruct(shape, jnp.bfloat16)


def params(mib):
    return pltpu.CompilerParams(vmem_limit_bytes=mib * MIB)


SIDES = {
    (0, 0): ((0, 0, 1), (0, 1, 1), (0, 0, 1), (1, 1, 1)),
    (0, 1): ((1, 0, 1), (1, 1, 1), (1, 0, 1), (0, 1, -1)),
    (1, 0): ((0, 1, 1), (0, 0, 1), (0, 1, -1), (1, 0, -1)),
    (1, 1): ((1, 1, 1), (1, 0, 1), (1, 1, -1), (0, 0, 1)),
}


def cut_kernel(values, chunks, orbitals):
    for e in range(8):
        chunks[e] = values[:, pl.ds(48 * e, 48)]
    orbitals[...] = values[:, :64]


def cut_values(values):
    return pl.pallas_call(
        cut_kernel,
        out_shape=(bf16(8, 16, 48, 128), bf16(16, 64, 128)),
        in_specs=[VMEM],
        out_specs=(VMEM, VMEM),
        compiler_params=params(8),
        cost_estimate=pl.CostEstimate(flops=0, bytes_accessed=3_000_000, transcendentals=0),
        name="cut_values",
    )(values)


def product_kernel(place, pattern, live, weight, low, own, high, mine, theirs, ext, sems):
    i = pl.program_id(0)

    @pl.when(i == 0)
    def _():
        copies = [
            pltpu.make_async_copy(src, ext.at[pl.ds(8 * n, 8)], sems.at[n]) for n, src in enumerate((low, own, high))
        ]
        for copy in copies:
            copy.start()
        for copy in copies:
            copy.wait()

    first = place[0]
    scale = weight[0]
    even = place[1] == 0
    orbital = lax.broadcasted_iota(jnp.int32, (64, 256), 1) % 64
    row = lax.broadcasted_iota(jnp.int32, (64, 256), 0)
    columns = [pattern[i, k] for k in range(6)]
    total = None
    own_pieces = {(part, spin): ext[8 + i, part, pl.ds(64 * spin, 64), :] for part in range(2) for spin in range(2)}
    for (spin, part), rows in SIDES.items():
        side = jnp.concatenate([own_pieces[p, s] if sign == 1 else -own_pieces[p, s] for p, s, sign in rows], axis=0)
        left = jnp.concatenate([ext[c - first + 8, part, pl.ds(spin * 64, 64), :] for c in columns], axis=0)
        term = lax.dot_general(left, side, NT, preferred_element_type=jnp.float32)
        total = term if total is None else total + term
    kept_row = orbital < live[first + i]
    pieces = []
    for k, c in enumerate(columns):
        kept = kept_row & (row < live[c])
        pieces.append(jnp.where(kept, total[64 * k : 64 * k + 64] * scale, 0.0))
    chunks = jnp.concatenate(pieces, axis=0).reshape(4, 2, 48, 256)
    mine[:, 0] = jnp.where(even, chunks[:, 0], chunks[:, 1]).astype(jnp.bfloat16)
    theirs[:, 0] = jnp.where(even, chunks[:, 1], chunks[:, 0]).astype(jnp.bfloat16)


def products(place, pattern, live, weight, low, own, high):
    by_block = pl.BlockSpec((4, 1, 48, 256), lambda i: (0, i, 0, 0))
    return pl.pallas_call(
        product_kernel,
        grid=(8,),
        out_shape=(bf16(4, 8, 48, 256),) * 2,
        in_specs=[SMEM] * 4 + [ANY] * 3,
        out_specs=(by_block, by_block),
        scratch_shapes=[pltpu.VMEM((24, 2, 128, 256), jnp.bfloat16), pltpu.SemaphoreType.DMA((3,))],
        compiler_params=params(56),
        cost_estimate=pl.CostEstimate(flops=1_600_000_000, bytes_accessed=9_000_000, transcendentals=0),
        name="products",
    )(place, pattern, live, weight, low, own, high)


def pair_kernel(place, landed, mine, got, *parts):
    for d in range(4):
        at = (place[2] + d) & 3
        parts[d][...] = (mine[at].astype(jnp.float32) + got[at].astype(jnp.float32)).astype(jnp.bfloat16)


def pair_sums(place, landed, mine, got):
    return pl.pallas_call(
        pair_kernel,
        out_shape=(bf16(8, 48, 256),) * 4,
        in_specs=[SMEM, ANY, VMEM, VMEM],
        out_specs=(VMEM,) * 4,
        compiler_params=params(6),
        cost_estimate=pl.CostEstimate(flops=400_000, bytes_accessed=2_400_000, transcendentals=0),
        name="pair_sums",
    )(place, landed, mine, got)


def apply_kernel(place, source, local, vals_q, own_o, other_o, *rest):
    count = len(rest) - 3
    shards, out, rows, sems = rest[:count], rest[count], rest[count + 1], rest[count + 2]
    e = pl.program_id(0)
    core, y_at, x_at, z_at = place[1], place[2], place[3], place[4]

    @pl.when(e == 0)
    def _():
        at, copies = 0, []
        for n, shard in enumerate(shards):
            size = shard.shape[0]
            copies.append(pltpu.make_async_copy(shard, rows.at[pl.ds(at, size)], sems.at[n]))
            at += size
        for copy in copies:
            copy.start()
        for copy in copies:
            copy.wait()

    device = e * 32 + 4 * z_at + x_at
    dy = (y_at - e // 2) & 3
    same = (e & 1) == core

    def run(values_o):
        total = jnp.zeros((4, 8, 128), jnp.float32)
        for r in range(16):
            request = device * 16 + r
            src = source[request]
            loc = local[request]
            dx = (x_at - src) & 3
            dz = (z_at - src // 4) & 7
            at = jnp.where(
                loc < SPLIT,
                SPLIT * (4 * dz + dx) + loc,
                32 * SPLIT + (8 - SPLIT) * (8 * dx + dz) + loc - SPLIT,
            )
            applied = lax.dot_general(rows[at], vals_q[0, r], TN, preferred_element_type=jnp.float32)
            weighted = applied.reshape(4, 8, 8, 128) * values_o[dy, r].astype(jnp.float32).reshape(1, 8, 8, 128)
            total = total + jnp.sum(weighted, axis=1)
        sums = jnp.sum(total, axis=1)
        for at, c in enumerate((0, 1, 3, 2)):
            out[0, pl.ds(c, 1)] = sums[at : at + 1]

    @pl.when(same)
    def _():
        run(own_o)

    @pl.when(jnp.logical_not(same))
    def _():
        run(other_o)


def applied_sums(place, source, local, vals_q, own_o, other_o, shards):
    return pl.pallas_call(
        apply_kernel,
        grid=(8,),
        out_shape=jax.ShapeDtypeStruct((8, 4, 128), jnp.float32),
        in_specs=[SMEM] * 3
        + [pl.BlockSpec((1, 16, 48, 128), lambda e: (e, 0, 0, 0)), VMEM, VMEM]
        + [ANY] * len(shards),
        out_specs=pl.BlockSpec((1, 4, 128), lambda e: (e, 0, 0)),
        scratch_shapes=[pltpu.VMEM((256, 48, 256), jnp.bfloat16), pltpu.SemaphoreType.DMA((len(shards),))],
        compiler_params=params(24),
        cost_estimate=pl.CostEstimate(flops=400_000_000, bytes_accessed=8_000_000, transcendentals=0),
        name="applied_sums",
    )(place, source, local, vals_q, own_o, other_o, *shards)


def shifted(value, axis, by):
    count = lax.axis_size(axis)
    return lax.ppermute(value, axis, [(n, (n + by) % count) for n in range(count)])


def gathered(value, axis):
    return [value] + [shifted(value, axis, d) for d in (1, 2, 3)]


def three_ways(value):
    ahead, behind, around = value, value, {0: value}
    for step in (1, 2, 3):
        ahead, behind = shifted(ahead, "z", 1), shifted(behind, "z", 7)
        around[step], around[8 - step] = ahead, behind
    return around, ahead, behind


def flat(value):
    return value.reshape((-1,) + value.shape[-2:])


def local_program(panels, energy_weight, block_orbitals, pattern_columns, request_source, request_local, orbital_values):
    core = lax.axis_index("core")
    y_at, z_at, x_at = lax.axis_index("y"), lax.axis_index("z"), lax.axis_index("x")
    place = jnp.stack([(z_at * 4 + x_at) * 8, core, y_at, x_at, z_at]).astype(jnp.int32)
    own = panels[0]
    swap = [(0, 1), (1, 0)]
    low = lax.ppermute(own, ("z", "x"), [(n, n + 1) for n in range(31)])
    high = lax.ppermute(own, ("z", "x"), [(n + 1, n) for n in range(31)])

    chunks, orbitals = cut_values(orbital_values)
    own_o = jnp.stack(gathered(orbitals, "y"))
    other_o = lax.ppermute(own_o, "core", swap)
    vals_q = lax.all_to_all(chunks, ("y", "core"), 0, 0, tiled=True)
    landed = jnp.stack([vals_q[0, 0, :8], own_o[1, 0, :8] + own_o[2, 0, :8] + own_o[3, 0, :8]])

    mine, theirs = products(place, pattern_columns, block_orbitals, energy_weight, low, own, high)
    got = lax.ppermute(theirs, "core", swap)
    parts = pair_sums(place, landed, mine, got)
    total = parts[0].astype(jnp.float32)
    for d in (1, 2, 3):
        total = total + shifted(parts[d], "y", d).astype(jnp.float32)
    total = total.astype(jnp.bfloat16)

    seconds, ahead, behind = three_ways(total[SPLIT:])
    seconds[4] = shifted(ahead, "z", 1)
    over_x = gathered(total[:SPLIT], "x")
    first = jnp.stack(over_x)
    second = jnp.stack([seconds[d] for d in range(8)])
    firsts, ahead, behind = three_ways(first)
    last = [shifted(ahead[:2], "z", 1), shifted(behind[2:], "z", 7)]
    shards = [firsts[d] for d in range(4)] + last + [firsts[d] for d in (5, 6, 7)]
    right, left = shifted(second, "x", 1), shifted(second, "x", 3)
    shards += [second, right, shifted(right[:4], "x", 1), shifted(left[4:], "x", 3), left]

    sums = applied_sums(
        place, request_source.reshape(-1), request_local, vals_q, own_o, other_o, [flat(s) for s in shards]
    )
    return jnp.sum(lax.all_to_all(sums, ("y", "core"), 0, 0, tiled=True), axis=0)


def solution(mesh):
    fine = Mesh(mesh.devices.reshape(4, 2, 8, 4), ("y", "core", "z", "x"))
    energy, rows = ("y", "core"), ("z", "x")
    in_specs = (
        P(energy, rows, None, None, None),
        P(energy),
        P(),
        P(rows, None),
        P(),
        P(),
        P(energy + rows, None, None),
    )
    return jax.shard_map(
        local_program, mesh=fine, in_specs=in_specs, out_specs=P(None, energy + rows), check_vma=False
    )
```
